32 devices in a mesh: corpus: 8 (over z, y), feat: 4 (over x, core).
Axes of the slice: x: 2, y: 2, z: 4, core: 2. Of those that a mesh axis runs over, the one named last changes fastest.
Arguments:
- slab: bfloat16 [4096, 7168], P('corpus', 'feat'), may hold values from -6 to 6
- factor: bfloat16 [7168, 7168], P('feat', 'corpus'), as said below
- queries: bfloat16 [128, 7168], P('corpus', 'feat'), may hold values from -0.0625 to 0.0625
Outputs:
- whitened: bfloat16 [4096, 7168], P('corpus', 'feat')
- scores: float32 [4096, 128], P(('corpus', 'feat'))
The draws below stay inside these ranges and needn't reach their ends.
Inputs may be any that keep to these rules, and one draw needn't show every extreme that they name: factor is lower triangular (zeros above the diagonal) and every diagonal entry is 1.2 or more.
All inputs are finite; a program needn't handle non-finite values.
Results may differ from the reference program's by a relative error of at most 0.0033.
Values may be sent and summed in bfloat16 or wider, within the bound.
A program may use at most 256 MiB of HBM per device.

```python
import jax
import jax.numpy as jnp
from jax import lax

BLK = 1792
F = 7168
EXAMPLES = 4096
QUERIES = 128
N_FEAT = 4


def draw_factor(key, part):
    base = jax.random.fold_in(key, 11)
    first_key, second_key = jax.random.split(base, 2)
    spread = jax.random.normal(first_key, (F, F), jnp.float32)
    diagonal_values = jax.random.uniform(second_key, (F,), jnp.float32, 1.5, 3.0)
    lower_part = jnp.tril(spread * (1.5 / jnp.sqrt(jnp.float32(F))), -1)
    return (lower_part + jnp.diag(diagonal_values)).astype(jnp.bfloat16)


def block_levels(stream_key, dims, pieces, smallest, high):
    def one(position, shards_of):
        heights = jax.random.uniform(jax.random.fold_in(jax.random.fold_in(stream_key, 6), position), (shards_of,), jnp.float32, smallest / len(pieces), high / len(pieces))
        return jnp.repeat(jnp.exp(heights), dims[position] // shards_of).reshape((-1,) + (1,) * (len(dims) - position - 1))

    loudness = one(*pieces[0])
    for cut in pieces[1:]:
        loudness = loudness * one(*cut)
    return loudness


def centred(own_key, extent, deviation, most, pieces=(), held_as=jnp.bfloat16):
    entries = jax.random.normal(own_key, extent, jnp.float32) * deviation
    if len(pieces) > 0:
        entries = block_levels(own_key, extent, pieces, -0.22, 0.18) * entries
    return jnp.clip(entries, min=-most, max=most).astype(held_as)


def setup_inputs(seed: int = 0) -> dict:
    splits = jax.random.split(jax.random.key(seed), 4)
    slab = centred(splits[0], (EXAMPLES, F), 1.0, 6.0, ((0, 8), (1, 4)))
    factor = draw_factor(jax.random.fold_in(splits[3], 71), 0)
    queries = centred(splits[2], (QUERIES, F), F ** -0.5, 0.0625, ((0, 8), (1, 4)))
    return {"slab": slab, "factor": factor, "queries": queries}


def right_product(left, right):
    return lax.dot_general(left.astype(jnp.float32), right.astype(jnp.float32), (((1,), (1,)), ((), ())), preferred_element_type=jnp.float32)

def reference(slab, factor, queries):
    solved_blocks = []
    for section in range(N_FEAT):
        lower_edge = section * BLK
        pending = slab[:, lower_edge:lower_edge + BLK].astype(jnp.float32)
        for earlier in range(section):
            coupling = factor[lower_edge:lower_edge + BLK, earlier * BLK:(earlier + 1) * BLK]
            pending = pending - right_product(solved_blocks[earlier], coupling)
        diagonal_block = factor[lower_edge:lower_edge + BLK, lower_edge:lower_edge + BLK].astype(jnp.float32)
        settled = jax.scipy.linalg.solve_triangular(diagonal_block, pending.T, lower=True).T
        solved_blocks.append(settled.astype(jnp.bfloat16))
    whitened = jnp.concatenate(solved_blocks, axis=1)
    scores = right_product(whitened, queries)
    return (whitened, scores)
```

```python
import jax
import jax.numpy as jnp
from jax import lax
from jax.sharding import PartitionSpec as P

BASE = 128
AXES = ("corpus", "feat")


def dot_t(left, right):
    return lax.dot_general(
        left, right, (((1,), (1,)), ((), ())), preferred_element_type=jnp.float32
    )


def split(value):
    high = lax.reduce_precision(value, 8, 7)
    return high.astype(jnp.bfloat16), (value - high).astype(jnp.bfloat16)


def exact(left, right):
    return jnp.matmul(
        left, right, precision=lax.Precision.HIGHEST, preferred_element_type=jnp.float32
    )


def inverse_of(lower):
    size = lower.shape[0]
    count = -(-size // BASE)
    padded = jnp.pad(lower, ((0, count * BASE - size),) * 2)
    blocks = jnp.stack(
        [padded[i * BASE : (i + 1) * BASE, i * BASE : (i + 1) * BASE] for i in range(count)]
    )
    row = lax.broadcasted_iota(jnp.int32, (BASE, BASE), 0)
    col = lax.broadcasted_iota(jnp.int32, (BASE, BASE), 1)
    position = lax.broadcasted_iota(jnp.int32, blocks.shape, 0) * BASE + row[None]
    on = (row == col)[None]
    inverse = jnp.where(on, 1.0 / jnp.where(on & (position < size), blocks, 1.0), 0.0)
    width = 1
    while width < BASE:
        below = (row // width % 2 == 1) & (row // width - 1 == col // width)
        joined = jnp.where(below[None], blocks, 0.0)
        inverse = inverse - exact(inverse, exact(joined, inverse))
        width *= 2
    parts = [(i * BASE, inverse[i]) for i in range(count)]
    while len(parts) > 1:
        merged = []
        for i in range(0, len(parts) - 1, 2):
            (start, a), (middle, b) = parts[i], parts[i + 1]
            na, nb = a.shape[0], b.shape[0]
            joined = padded[middle : middle + nb, start : start + na]
            corner = -exact(b, exact(joined, a))
            top = jnp.concatenate([a, jnp.zeros((na, nb), jnp.float32)], 1)
            bottom = jnp.concatenate([corner, b], 1)
            merged.append((start, jnp.concatenate([top, bottom], 0)))
        if len(parts) % 2:
            merged.append(parts[-1])
        parts = merged
    return parts[0][1][:size, :size]


def local(slab, factor, queries):
    c, f = lax.axis_index("corpus"), lax.axis_index("feat")
    n, k = lax.axis_size("corpus"), lax.axis_size("feat")
    rows, width = slab.shape
    piece = factor.shape[1]
    per = width // piece

    walk = list(range(0, n, 2)) + list(range(1, n, 2))[::-1]
    order = jnp.array(walk, jnp.int32)
    place = jnp.array([walk.index(i) for i in range(n)], jnp.int32)[c]

    def origin(step, sign):
        return order[(place - sign * step) % n]

    def hop(value, step, sign, wanted):
        pairs = []
        for p in range(n):
            start = walk[(p - sign * (step - 1)) % n]
            for g in range(k):
                if wanted(start, g):
                    pairs.append((walk[p] * k + g, walk[(p + sign) % n] * k + g))
        return lax.ppermute(value, AXES, pairs)

    def ring(value, wanted, place_in, last_sign):
        held = {1: value, -1: value}
        for step in range(1, n // 2 + 1):
            for sign in (1, -1):
                if 2 * step == n and sign != last_sign:
                    continue
                held[sign] = hop(held[sign], step, sign, wanted)
                place_in(held[sign], origin(step, sign))

    offset = c - f * per
    mine = (offset >= 0) & (offset < per)
    own = jnp.clip(offset, 0, per - 1)
    diagonal = lax.dynamic_slice_in_dim(factor, own * piece, piece, 0).astype(jnp.float32)
    diagonal = jnp.where(mine, diagonal, jnp.eye(piece, dtype=jnp.float32))
    high, low = split(inverse_of(diagonal))
    top = jnp.where(mine, high, factor[:piece])

    state = {
        "rows": jnp.zeros((width, n * piece), jnp.bfloat16),
        "low": jnp.zeros((per + 1, piece, piece), jnp.bfloat16),
        "queries": jnp.zeros((n,) + queries.shape, jnp.bfloat16),
    }

    def put_top(value, start):
        state["rows"] = lax.dynamic_update_slice(state["rows"], value, (0, start * piece))

    def put_rest(value, start):
        state["rows"] = lax.dynamic_update_slice(state["rows"], value, (piece, start * piece))

    def put_low(value, start):
        slot = start - f * per
        slot = jnp.where((slot >= 0) & (slot < per), slot, per)
        state["low"] = lax.dynamic_update_slice(state["low"], value[None], (slot, 0, 0))

    def put_queries(value, start):
        state["queries"] = lax.dynamic_update_slice(state["queries"], value[None], (start, 0, 0))

    if per > 1:
        put_rest(factor[piece:], c)
        ring(factor[piece:], lambda s, g: s < g * per + per - 1, put_rest, 1)
    put_queries(queries, c)
    ring(queries, lambda s, g: True, put_queries, 1)
    put_top(top, c)
    ring(top, lambda s, g: s < g * per + per, put_top, -1)
    put_low(low, c)
    ring(low, lambda s, g: g * per <= s < g * per + per, put_low, 1)
    gathered, lows = state["rows"], state["low"]
    all_queries = state["queries"].reshape(n * queries.shape[0], width)

    def settle(pending, gathered, lows):
        block = lax.dynamic_slice_in_dim(gathered, f * width, width, 1)
        solved, parts = [], []
        for h in range(per):
            value = pending[:, h * piece : (h + 1) * piece]
            for g in range(h):
                coupling = block[h * piece : (h + 1) * piece, g * piece : (g + 1) * piece]
                value = value - (dot_t(parts[g][0], coupling) + dot_t(parts[g][1], coupling))
            value_high, value_low = split(value)
            inverse_high = block[:piece, h * piece : (h + 1) * piece]
            result = dot_t(value_high, inverse_high) + (
                dot_t(value_low, inverse_high) + dot_t(value_high, lows[h])
            )
            parts.append(split(result))
            solved.append(parts[-1][0])
        return jnp.concatenate(solved, 1)

    pending = [slab.astype(jnp.float32)] * k
    solved = jnp.zeros_like(slab)
    for section in range(k):
        solved = lax.cond(
            f == section,
            lambda v: settle(v[0], v[1], v[2]),
            lambda v: v[3],
            (pending[section], gathered, lows, solved),
        )
        arrived = solved
        for later in range(section + 1, k):
            pairs = [(i * k + later - 1, i * k + later) for i in range(n)]
            arrived = lax.ppermute(arrived, AXES, pairs)
            coupling = gathered[:, section * width : (section + 1) * width]
            pending[later] = lax.cond(
                f == later,
                lambda v: v[0] - dot_t(v[1], v[2]),
                lambda v: v[0],
                (pending[later], arrived, coupling),
            )
    partial = dot_t(solved, all_queries)
    share = rows // k
    scores = lax.dynamic_slice_in_dim(partial, f * share, share, 0)
    for turn in range(1, k):
        outgoing = lax.dynamic_slice_in_dim(partial, (f + turn) % k * share, share, 0)
        pairs = [(i * k + g, i * k + (g + turn) % k) for i in range(n) for g in range(k)]
        scores = scores + lax.ppermute(outgoing, AXES, pairs)
    return (solved, scores)


def solution(mesh):
    return jax.shard_map(
        local,
        mesh=mesh,
        in_specs=(P("corpus", "feat"), P("feat", "corpus"), P("corpus", "feat")),
        out_specs=(P("corpus", "feat"), P(("corpus", "feat"), None)),
        check_vma=False,
    )
```

```python
import functools

import jax
import jax.numpy as jnp
from jax import lax
from jax.experimental import pallas as pl
from jax.experimental.pallas import tpu as pltpu
from jax.sharding import PartitionSpec as P

BASE = 128
AXES = ("corpus", "feat")


def dot_t(left, right):
    return lax.dot_general(
        left, right, (((1,), (1,)), ((), ())), preferred_element_type=jnp.float32
    )


def split(value):
    high = lax.reduce_precision(value, 8, 7)
    return high.astype(jnp.bfloat16), (value - high).astype(jnp.bfloat16)


def exact(left, right):
    return jnp.matmul(
        left, right, precision=lax.Precision.HIGHEST, preferred_element_type=jnp.float32
    )


def inverse_of(lower):
    size = lower.shape[0]
    count = -(-size // BASE)
    padded = jnp.pad(lower, ((0, count * BASE - size),) * 2)
    blocks = jnp.stack(
        [padded[i * BASE : (i + 1) * BASE, i * BASE : (i + 1) * BASE] for i in range(count)]
    )
    row = lax.broadcasted_iota(jnp.int32, (BASE, BASE), 0)
    col = lax.broadcasted_iota(jnp.int32, (BASE, BASE), 1)
    position = lax.broadcasted_iota(jnp.int32, blocks.shape, 0) * BASE + row[None]
    on = (row == col)[None]
    inverse = jnp.where(on, 1.0 / jnp.where(on & (position < size), blocks, 1.0), 0.0)
    width = 1
    while width < BASE:
        below = (row // width % 2 == 1) & (row // width - 1 == col // width)
        joined = jnp.where(below[None], blocks, 0.0)
        inverse = inverse - exact(inverse, exact(joined, inverse))
        width *= 2
    parts = [(i * BASE, inverse[i]) for i in range(count)]
    while len(parts) > 1:
        merged = []
        for i in range(0, len(parts) - 1, 2):
            (start, a), (middle, b) = parts[i], parts[i + 1]
            na, nb = a.shape[0], b.shape[0]
            joined = padded[middle : middle + nb, start : start + na]
            corner = -exact(b, exact(joined, a))
            top = jnp.concatenate([a, jnp.zeros((na, nb), jnp.float32)], 1)
            bottom = jnp.concatenate([corner, b], 1)
            merged.append((start, jnp.concatenate([top, bottom], 0)))
        if len(parts) % 2:
            merged.append(parts[-1])
        parts = merged
    return parts[0][1][:size, :size]


REST, TOP, LOW, ASK = range(4)
CHUNKS = 2


def kernel(
    n, k, slab, factor, top, low, ask, solved, scores,
    rows_of, lows, asks, pending, extra, arrived, shares, summed,
    own_sem, send_sem, recv_sem, chain_send, chain_recv, score_send, score_recv,
):
    c, f = lax.axis_index("corpus"), lax.axis_index("feat")
    per, rows, piece = slab.shape
    half = n // 2
    chunk = rows // CHUNKS
    share = rows // k
    place = jnp.where(c % 2 == 0, c // 2, n - 1 - c // 2)

    def at(position):
        q = (position + 2 * n) % n
        return jnp.where(q < half, 2 * q, 2 * (n - 1 - q) + 1)

    after, before = at(place + 1), at(place - 1)

    barrier = pltpu.get_barrier_semaphore()
    for other in (after, before):
        pl.semaphore_signal(barrier, 1, device_id=(other, f), device_id_type=pl.DeviceIdType.MESH)
    for turn in range(1, k):
        pl.semaphore_signal(
            barrier, 1, device_id=(c, (f + turn) % k), device_id_type=pl.DeviceIdType.MESH
        )
    pl.semaphore_wait(barrier, k + 1)

    def exists(kind, start):
        if kind == REST:
            return start < f * per + per - 1
        if kind == TOP:
            return start < f * per + per
        if kind == LOW:
            return (start >= f * per) & (start < f * per + per)
        return start >= 0

    def slot(kind, start):
        if kind == REST:
            return rows_of.at[start, pl.ds(piece, (per - 1) * piece)]
        if kind == TOP:
            return rows_of.at[start, pl.ds(0, piece)]
        if kind == LOW:
            return lows.at[start - f * per]
        return asks.at[start]

    source = {REST: factor.at[pl.ds(piece, (per - 1) * piece)], TOP: top, LOW: low, ASK: ask}
    kinds = (TOP, LOW, REST, ASK) if per > 1 else (TOP, LOW, ASK)

    def reach(kind, way):
        right = n - 1 - half if kind == TOP else half
        return right if way == 0 else n - 1 - right

    def copy(kind, way, start, step, src):
        return pltpu.make_async_remote_copy(
            src_ref=src,
            dst_ref=slot(kind, start),
            send_sem=send_sem.at[kind, way, step],
            recv_sem=recv_sem.at[kind, start],
            device_id=(after if way == 0 else before, f),
            device_id_type=pl.DeviceIdType.MESH,
        )

    def mine(kind):
        return pltpu.make_async_copy(source[kind], slot(kind, c), own_sem.at[kind])

    for kind in kinds:
        @pl.when(exists(kind, c))
        def _(kind=kind):
            for way in (0, 1):
                copy(kind, way, c, 0, source[kind]).start()
            mine(kind).start()

    def forward(step, carry):
        for kind in kinds:
            for way in (0, 1):
                start = at(place - step if way == 0 else place + step)

                @pl.when(exists(kind, start) & (step < reach(kind, way)))
                def _(kind=kind, way=way, start=start):
                    moved = copy(kind, way, start, step, slot(kind, start))
                    moved.wait_recv()
                    moved.start()
        return carry

    lax.fori_loop(1, half, forward, 0)
    for h in range(per):
        pending[h] = slab[h].astype(jnp.float32)

    def ready(kind, start):
        last = (start == at(place - reach(kind, 0))) | (start == at(place + reach(kind, 1)))

        @pl.when(exists(kind, start) & last & (start != c))
        def _():
            copy(kind, 0, start, 0, slot(kind, start)).wait_recv()

        @pl.when(exists(kind, start) & (start == c))
        def _():
            mine(kind).wait()

    def section_ready(s, with_low):
        for g in range(per):
            for kind in kinds:
                if kind == TOP or kind == REST or (kind == LOW and with_low):
                    ready(kind, s * per + g)

    def lines(r):
        return pl.ds(pl.multiple_of(r * chunk, chunk), chunk)

    def chain(s, r, to):
        return pltpu.make_async_remote_copy(
            src_ref=solved.at[:, lines(r)],
            dst_ref=arrived.at[s, :, lines(r)],
            send_sem=chain_send.at[to, r],
            recv_sem=chain_recv.at[s, r],
            device_id=(c, to),
            device_id_type=pl.DeviceIdType.MESH,
        )

    def update(s, r):
        chain(s, r, (f + 1) % k).wait_recv()

        def into(h, carry):
            below = pl.ds(pl.multiple_of(h * piece, piece), piece)
            total = pending[h, lines(r)]
            for g in range(per):
                total = total - dot_t(arrived[s, g, lines(r)], rows_of[s * per + g, below])
            pending[h, lines(r)] = total
            return carry

        lax.fori_loop(0, per, into, 0)

    def halves(value):
        high = value.astype(jnp.bfloat16)
        return high, (value - high.astype(jnp.float32)).astype(jnp.bfloat16)

    def settle(r):
        for h in range(per):
            value = pending[h, lines(r)]
            for g in range(h):
                coupling = rows_of[f * per + g, h * piece : (h + 1) * piece]
                value = value - dot_t(solved[g, lines(r)], coupling)
                value = value - dot_t(extra[g], coupling)
            high, rest = halves(value)
            inverse = rows_of[f * per + h, :piece]
            result = dot_t(rest, inverse) + dot_t(high, lows[h])
            result = result + dot_t(high, inverse)
            high, rest = halves(result)
            solved[h, lines(r)] = high
            extra[h] = rest

    def early(s, carry):
        @pl.when(s < f)
        def _():
            section_ready(s, False)

            @pl.when(s < f - 1)
            def _():
                def each(r, inner):
                    update(s, r)
                    return inner

                lax.fori_loop(0, CHUNKS, each, 0)

        return carry

    lax.fori_loop(0, k - 1, early, 0)
    section_ready(f, True)

    def step(r, carry):
        @pl.when(f > 0)
        def _():
            update(f - 1, r)

        settle(r)
        for to in range(1, k):
            @pl.when(to > f)
            def _(to=to):
                chain(f, r, to).start()
        return carry

    lax.fori_loop(0, CHUNKS, step, 0)

    def asked(start, carry):
        ready(ASK, start)
        return carry

    lax.fori_loop(0, n, asked, 0)

    def give(j):
        return pltpu.make_async_remote_copy(
            src_ref=shares.at[j],
            dst_ref=summed.at[f],
            send_sem=score_send.at[j],
            recv_sem=score_recv.at[f],
            device_id=(c, j),
            device_id_type=pl.DeviceIdType.MESH,
        )

    def take(j):
        return pltpu.make_async_remote_copy(
            src_ref=shares.at[j],
            dst_ref=summed.at[j],
            send_sem=score_send.at[j],
            recv_sem=score_recv.at[j],
            device_id=(c, j),
            device_id_type=pl.DeviceIdType.MESH,
        )

    for j in range(k):
        total = jnp.zeros(scores.shape, jnp.float32)
        for h in range(per):
            every = asks[:, h].reshape(scores.shape[1], piece)
            total = total + dot_t(solved[h, j * share : (j + 1) * share], every)
        shares[j] = total

        @pl.when(f != j)
        def _(j=j):
            give(j).start()

    total = shares[f]
    for turn in range(1, k):
        other = (f + turn) % k
        take(other).wait_recv()
        total = total + summed[other]
    scores[...] = total

    for j in range(k):
        @pl.when(f != j)
        def _(j=j):
            give(j).wait_send()

    def sent(r, carry):
        for to in range(1, k):
            @pl.when(to > f)
            def _(to=to):
                chain(f, r, to).wait_send()
        return carry

    lax.fori_loop(0, CHUNKS, sent, 0)
    for kind in kinds:
        @pl.when(exists(kind, c))
        def _(kind=kind):
            for way in (0, 1):
                copy(kind, way, c, 0, source[kind]).wait_send()

    def forwarded(step, carry):
        for kind in kinds:
            for way in (0, 1):
                start = at(place - step if way == 0 else place + step)

                @pl.when(exists(kind, start) & (step < reach(kind, way)))
                def _(kind=kind, way=way, start=start):
                    copy(kind, way, start, step, slot(kind, start)).wait_send()
        return carry

    lax.fori_loop(1, half, forwarded, 0)


def local(slab, factor, queries):
    c, f = lax.axis_index("corpus"), lax.axis_index("feat")
    n, k = lax.axis_size("corpus"), lax.axis_size("feat")
    rows, width = slab.shape
    piece = factor.shape[1]
    per = width // piece
    asked = queries.shape[0]

    offset = c - f * per
    mine = (offset >= 0) & (offset < per)
    own = jnp.clip(offset, 0, per - 1)
    diagonal = lax.dynamic_slice_in_dim(factor, own * piece, piece, 0).astype(jnp.float32)
    diagonal = jnp.where(mine, diagonal, jnp.eye(piece, dtype=jnp.float32))
    high, low = split(inverse_of(diagonal))
    top = jnp.where(mine, high, factor[:piece])

    def cut(value):
        return value.reshape(value.shape[0], per, piece).transpose(1, 0, 2)

    vmem = pl.BlockSpec(memory_space=pltpu.VMEM)
    anywhere = pl.BlockSpec(memory_space=pl.ANY)
    half = n // 2
    solved, scores = pl.pallas_call(
        functools.partial(kernel, n, k),
        out_shape=(
            jax.ShapeDtypeStruct((per, rows, piece), jnp.bfloat16),
            jax.ShapeDtypeStruct((rows // k, n * asked), jnp.float32),
        ),
        in_specs=[vmem, anywhere, anywhere, anywhere, anywhere],
        out_specs=(vmem, vmem),
        scratch_shapes=[
            pltpu.VMEM((n, width, piece), jnp.bfloat16),
            pltpu.VMEM((per, piece, piece), jnp.bfloat16),
            pltpu.VMEM((n, per, asked, piece), jnp.bfloat16),
            pltpu.VMEM((per, rows, piece), jnp.float32),
            pltpu.VMEM((per, rows // CHUNKS, piece), jnp.bfloat16),
            pltpu.VMEM((k - 1, per, rows, piece), jnp.bfloat16),
            pltpu.VMEM((k, rows // k, n * asked), jnp.float32),
            pltpu.VMEM((k, rows // k, n * asked), jnp.float32),
            pltpu.SemaphoreType.DMA((4,)),
            pltpu.SemaphoreType.DMA((4, 2, half)),
            pltpu.SemaphoreType.DMA((4, n)),
            pltpu.SemaphoreType.DMA((k, CHUNKS)),
            pltpu.SemaphoreType.DMA((k - 1, CHUNKS)),
            pltpu.SemaphoreType.DMA((k,)),
            pltpu.SemaphoreType.DMA((k,)),
        ],
        compiler_params=pltpu.CompilerParams(
            collective_id=0, has_side_effects=True, vmem_limit_bytes=60 * 1024 * 1024
        ),
    )(cut(slab), factor, top, low, cut(queries))
    return (solved.transpose(1, 0, 2).reshape(rows, width), scores)


def solution(mesh):
    return jax.shard_map(
        local,
        mesh=mesh,
        in_specs=(P("corpus", "feat"), P("feat", "corpus"), P("corpus", "feat")),
        out_specs=(P("corpus", "feat"), P(("corpus", "feat"), None)),
        check_vma=False,
    )
```

```python
import functools

import jax
import jax.numpy as jnp
from jax import lax
from jax.experimental import pallas as pl
from jax.experimental.pallas import tpu as pltpu
from jax.sharding import PartitionSpec as P

BASE = 128
AXES = ("corpus", "feat")


def dot_t(left, right):
    return lax.dot_general(
        left, right, (((1,), (1,)), ((), ())), preferred_element_type=jnp.float32
    )


def split(value):
    high = lax.reduce_precision(value, 8, 7)
    return high.astype(jnp.bfloat16), (value - high).astype(jnp.bfloat16)


def exact(left, right):
    return jnp.matmul(
        left, right, precision=lax.Precision.HIGHEST, preferred_element_type=jnp.float32
    )


def inverse_of(lower):
    size = lower.shape[0]
    count = -(-size // BASE)
    padded = jnp.pad(lower, ((0, count * BASE - size),) * 2)
    blocks = jnp.stack(
        [padded[i * BASE : (i + 1) * BASE, i * BASE : (i + 1) * BASE] for i in range(count)]
    )
    row = lax.broadcasted_iota(jnp.int32, (BASE, BASE), 0)
    col = lax.broadcasted_iota(jnp.int32, (BASE, BASE), 1)
    position = lax.broadcasted_iota(jnp.int32, blocks.shape, 0) * BASE + row[None]
    on = (row == col)[None]
    inverse = jnp.where(on, 1.0 / jnp.where(on & (position < size), blocks, 1.0), 0.0)
    width = 1
    while width < BASE:
        below = (row // width % 2 == 1) & (row // width - 1 == col // width)
        joined = jnp.where(below[None], blocks, 0.0)
        inverse = inverse - exact(inverse, exact(joined, inverse))
        width *= 2
    parts = [(i * BASE, inverse[i]) for i in range(count)]
    while len(parts) > 1:
        merged = []
        for i in range(0, len(parts) - 1, 2):
            (start, a), (middle, b) = parts[i], parts[i + 1]
            na, nb = a.shape[0], b.shape[0]
            joined = padded[middle : middle + nb, start : start + na]
            corner = -exact(b, exact(joined, a))
            top = jnp.concatenate([a, jnp.zeros((na, nb), jnp.float32)], 1)
            bottom = jnp.concatenate([corner, b], 1)
            merged.append((start, jnp.concatenate([top, bottom], 0)))
        if len(parts) % 2:
            merged.append(parts[-1])
        parts = merged
    return parts[0][1][:size, :size]


REST, TOP, LOW, ASK, RELAY = range(5)
CHUNKS = 2


def kernel(
    n, k, slab, factor, top, low, ask, solved, scores,
    rows_of, lows, asks, pending, extra, arrived, shares, summed,
    own_sem, send_sem, recv_sem, relay_send, pass_send, chain_send, chain_recv, score_send, score_recv,
):
    c, f = lax.axis_index("corpus"), lax.axis_index("feat")
    per, rows, piece = slab.shape
    half = n // 2
    chunk = rows // CHUNKS
    share = rows // k
    relayed = k == 4 and per > 1
    hub, goal = k - 1 - k // 2, k - 1
    place = jnp.where(c % 2 == 0, c // 2, n - 1 - c // 2)

    def at(position):
        q = (position + 2 * n) % n
        return jnp.where(q < half, 2 * q, 2 * (n - 1 - q) + 1)

    after, before = at(place + 1), at(place - 1)

    barrier = pltpu.get_barrier_semaphore()
    for other in (after, before):
        pl.semaphore_signal(barrier, 1, device_id=(other, f), device_id_type=pl.DeviceIdType.MESH)
    for turn in range(1, k):
        pl.semaphore_signal(
            barrier, 1, device_id=(c, (f + turn) % k), device_id_type=pl.DeviceIdType.MESH
        )
    pl.semaphore_wait(barrier, k + 1)

    def exists(kind, start):
        if kind == REST:
            return start < f * per + per - 1
        if kind == TOP:
            return start < f * per + per
        if kind == LOW:
            return (start >= f * per) & (start < f * per + per)
        return start >= 0

    def travels(kind, start):
        if kind == RELAY:
            return (start >= 0) & (f == hub)
        if kind == TOP and relayed:
            return exists(kind, start) & (f != goal)
        return exists(kind, start)

    def slot(kind, start):
        if kind == REST:
            return rows_of.at[start, pl.ds(piece, (per - 1) * piece)]
        if kind == TOP:
            return rows_of.at[start, pl.ds(0, piece)]
        if kind == LOW:
            return lows.at[start - f * per]
        if kind == RELAY:
            index = jnp.where(start < half, start + half, start)
            offset = pl.multiple_of(jnp.where(start < half, piece, 0), piece)
            return rows_of.at[index, pl.ds(offset, piece)]
        return asks.at[start]

    source = {REST: factor.at[pl.ds(piece, (per - 1) * piece)], TOP: top, LOW: low, ASK: ask}
    kinds = (TOP, LOW, REST, ASK) if per > 1 else (TOP, LOW, ASK)

    def place_of(start):
        return jnp.where(start % 2 == 0, start // 2, n - 1 - start // 2)

    def reach(kind, way, start):
        right = half - (place_of(start) + (kind == TOP)) % 2
        return right if way == 0 else n - 1 - right

    def is_last(kind, start):
        distance = (place - place_of(start) + n) % n
        right = reach(kind, 0, start)
        return (distance == right) | (distance == right + 1)

    def copy(kind, way, start, step, src):
        return pltpu.make_async_remote_copy(
            src_ref=src,
            dst_ref=slot(kind, start),
            send_sem=send_sem.at[kind, way, step],
            recv_sem=recv_sem.at[kind, start],
            device_id=(after if way == 0 else before, f),
            device_id_type=pl.DeviceIdType.MESH,
        )

    def mine(kind):
        return pltpu.make_async_copy(source[kind], slot(kind, c), own_sem.at[kind])

    def to_hub():
        return pltpu.make_async_remote_copy(
            src_ref=top,
            dst_ref=slot(RELAY, c),
            send_sem=relay_send.at[c],
            recv_sem=recv_sem.at[RELAY, c],
            device_id=(c, hub),
            device_id_type=pl.DeviceIdType.MESH,
        )

    def to_goal(start):
        return pltpu.make_async_remote_copy(
            src_ref=slot(RELAY, start),
            dst_ref=slot(TOP, start),
            send_sem=relay_send.at[start],
            recv_sem=recv_sem.at[TOP, start],
            device_id=(c, goal),
            device_id_type=pl.DeviceIdType.MESH,
        )

    if relayed:
        @pl.when(f == goal)
        def _():
            to_hub().start()

    for kind in kinds:
        @pl.when(travels(kind, c))
        def _(kind=kind):
            for way in (0, 1):
                copy(kind, way, c, 0, source[kind]).start()

        @pl.when(exists(kind, c))
        def _(kind=kind):
            mine(kind).start()

    if relayed:
        @pl.when(f == hub)
        def _():
            to_hub().wait_recv()
            for way in (0, 1):
                copy(RELAY, way, c, 0, slot(RELAY, c)).start()

    moving = kinds + ((RELAY,) if relayed else ())

    def forward(step, carry):
        for kind in moving:
            for way in (0, 1):
                start = at(place - step if way == 0 else place + step)

                @pl.when(travels(kind, start) & (step < reach(kind, way, start)))
                def _(kind=kind, way=way, start=start):
                    moved = copy(kind, way, start, step, slot(kind, start))
                    moved.wait_recv()
                    moved.start()
                    if kind == RELAY:
                        to_goal(start).start()
        return carry

    lax.fori_loop(1, half, forward, 0)
    for h in range(per):
        pending[h] = slab[h].astype(jnp.float32)

    def ready(kind, start):
        last = is_last(kind, start)
        if kind == TOP and relayed:
            last = last | (f == goal)

        @pl.when(exists(kind, start) & last & (start != c))
        def _():
            copy(kind, 0, start, 0, slot(kind, start)).wait_recv()

        @pl.when(exists(kind, start) & (start == c))
        def _():
            mine(kind).wait()

    def section_ready(s, with_low):
        for g in range(per):
            for kind in kinds:
                if kind == TOP or kind == REST or (kind == LOW and with_low):
                    ready(kind, s * per + g)

    def lines(r):
        return pl.ds(pl.multiple_of(r * chunk, chunk), chunk)

    def chain(s, r, to):
        return pltpu.make_async_remote_copy(
            src_ref=solved.at[:, lines(r)],
            dst_ref=arrived.at[s, :, lines(r)],
            send_sem=chain_send.at[to, r],
            recv_sem=chain_recv.at[s, r],
            device_id=(c, to),
            device_id_type=pl.DeviceIdType.MESH,
        )

    def update(s, r):
        chain(s, r, (f + 1) % k).wait_recv()

        def into(h, carry):
            below = pl.ds(pl.multiple_of(h * piece, piece), piece)
            total = pending[h, lines(r)]
            for g in range(per):
                total = total - dot_t(arrived[s, g, lines(r)], rows_of[s * per + g, below])
            pending[h, lines(r)] = total
            return carry

        lax.fori_loop(0, per, into, 0)

    def halves(value):
        high = value.astype(jnp.bfloat16)
        return high, (value - high.astype(jnp.float32)).astype(jnp.bfloat16)

    def settle(r):
        for h in range(per):
            value = pending[h, lines(r)]
            for g in range(h):
                coupling = rows_of[f * per + g, h * piece : (h + 1) * piece]
                value = value - dot_t(solved[g, lines(r)], coupling)
                value = value - dot_t(extra[g], coupling)
            high, rest = halves(value)
            inverse = rows_of[f * per + h, :piece]
            result = dot_t(rest, inverse) + dot_t(high, lows[h])
            result = result + dot_t(high, inverse)
            high, rest = halves(result)
            solved[h, lines(r)] = high
            extra[h] = rest

    def pass_on(r):
        return pltpu.make_async_remote_copy(
            src_ref=arrived.at[0, :, lines(r)],
            dst_ref=arrived.at[0, :, lines(r)],
            send_sem=pass_send.at[r],
            recv_sem=chain_recv.at[0, r],
            device_id=(c, goal),
            device_id_type=pl.DeviceIdType.MESH,
        )

    def passes(s):
        return (s == 0) & (f == goal - 1)

    def direct(to):
        if relayed and to == goal:
            return (f > 0) & (f < to)
        return f < to

    def early(s, carry):
        @pl.when(s < f)
        def _():
            section_ready(s, False)

            @pl.when(s < f - 1)
            def _():
                def each(r, inner):
                    update(s, r)
                    if relayed:
                        @pl.when(passes(s))
                        def _():
                            pass_on(r).start()

                    return inner

                lax.fori_loop(0, CHUNKS, each, 0)

        return carry

    lax.fori_loop(0, k - 1, early, 0)
    section_ready(f, True)

    def step(r, carry):
        @pl.when(f > 0)
        def _():
            update(f - 1, r)

        settle(r)
        for to in range(1, k):
            @pl.when(direct(to))
            def _(to=to):
                chain(f, r, to).start()
        return carry

    lax.fori_loop(0, CHUNKS, step, 0)

    def finish(start, carry):
        @pl.when((f == hub) & is_last(RELAY, start) & (start != c))
        def _():
            landed = copy(RELAY, 0, start, 0, slot(RELAY, start))
            landed.wait_recv()
            to_goal(start).start()

        return carry

    if relayed:
        lax.fori_loop(0, n, finish, 0)

    def asked(start, carry):
        ready(ASK, start)
        return carry

    lax.fori_loop(0, n, asked, 0)

    def give(j):
        return pltpu.make_async_remote_copy(
            src_ref=shares.at[j],
            dst_ref=summed.at[f],
            send_sem=score_send.at[j],
            recv_sem=score_recv.at[f],
            device_id=(c, j),
            device_id_type=pl.DeviceIdType.MESH,
        )

    def take(j):
        return pltpu.make_async_remote_copy(
            src_ref=shares.at[j],
            dst_ref=summed.at[j],
            send_sem=score_send.at[j],
            recv_sem=score_recv.at[j],
            device_id=(c, j),
            device_id_type=pl.DeviceIdType.MESH,
        )

    for j in range(k):
        total = jnp.zeros(scores.shape, jnp.float32)
        for h in range(per):
            every = asks[:, h].reshape(scores.shape[1], piece)
            total = total + dot_t(solved[h, j * share : (j + 1) * share], every)
        shares[j] = total

        @pl.when(f != j)
        def _(j=j):
            give(j).start()

    total = shares[f]
    for turn in range(1, k):
        other = (f + turn) % k
        take(other).wait_recv()
        total = total + summed[other]
    scores[...] = total

    for j in range(k):
        @pl.when(f != j)
        def _(j=j):
            give(j).wait_send()

    def sent(r, carry):
        for to in range(1, k):
            @pl.when(direct(to))
            def _(to=to):
                chain(f, r, to).wait_send()
        return carry

    lax.fori_loop(0, CHUNKS, sent, 0)
    for kind in kinds:
        @pl.when(travels(kind, c))
        def _(kind=kind):
            for way in (0, 1):
                copy(kind, way, c, 0, source[kind]).wait_send()

    if relayed:
        @pl.when(f == goal)
        def _():
            to_hub().wait_send()

        @pl.when(f == hub)
        def _():
            for way in (0, 1):
                copy(RELAY, way, c, 0, slot(RELAY, c)).wait_send()

        @pl.when(f == goal - 1)
        def _():
            for r in range(CHUNKS):
                pass_on(r).wait_send()

        def relayed_out(start, carry):
            @pl.when((f == hub) & (start != c))
            def _():
                to_goal(start).wait_send()

            return carry

        lax.fori_loop(0, n, relayed_out, 0)

    def forwarded(step, carry):
        for kind in moving:
            for way in (0, 1):
                start = at(place - step if way == 0 else place + step)

                @pl.when(travels(kind, start) & (step < reach(kind, way, start)))
                def _(kind=kind, way=way, start=start):
                    copy(kind, way, start, step, slot(kind, start)).wait_send()
        return carry

    lax.fori_loop(1, half, forwarded, 0)


def local(slab, factor, queries):
    c, f = lax.axis_index("corpus"), lax.axis_index("feat")
    n, k = lax.axis_size("corpus"), lax.axis_size("feat")
    rows, width = slab.shape
    piece = factor.shape[1]
    per = width // piece
    asked = queries.shape[0]

    offset = c - f * per
    mine = (offset >= 0) & (offset < per)
    own = jnp.clip(offset, 0, per - 1)
    diagonal = lax.dynamic_slice_in_dim(factor, own * piece, piece, 0).astype(jnp.float32)
    diagonal = jnp.where(mine, diagonal, jnp.eye(piece, dtype=jnp.float32))
    high, low = split(inverse_of(diagonal))
    top = jnp.where(mine, high, factor[:piece])

    def cut(value):
        return value.reshape(value.shape[0], per, piece).transpose(1, 0, 2)

    vmem = pl.BlockSpec(memory_space=pltpu.VMEM)
    anywhere = pl.BlockSpec(memory_space=pl.ANY)
    half = n // 2
    solved, scores = pl.pallas_call(
        functools.partial(kernel, n, k),
        out_shape=(
            jax.ShapeDtypeStruct((per, rows, piece), jnp.bfloat16),
            jax.ShapeDtypeStruct((rows // k, n * asked), jnp.float32),
        ),
        in_specs=[vmem, anywhere, anywhere, anywhere, anywhere],
        out_specs=(vmem, vmem),
        scratch_shapes=[
            pltpu.VMEM((n, width, piece), jnp.bfloat16),
            pltpu.VMEM((per, piece, piece), jnp.bfloat16),
            pltpu.VMEM((n, per, asked, piece), jnp.bfloat16),
            pltpu.VMEM((per, rows, piece), jnp.float32),
            pltpu.VMEM((per, rows // CHUNKS, piece), jnp.bfloat16),
            pltpu.VMEM((k - 1, per, rows, piece), jnp.bfloat16),
            pltpu.VMEM((k, rows // k, n * asked), jnp.float32),
            pltpu.VMEM((k, rows // k, n * asked), jnp.float32),
            pltpu.SemaphoreType.DMA((4,)),
            pltpu.SemaphoreType.DMA((5, 2, half)),
            pltpu.SemaphoreType.DMA((5, n)),
            pltpu.SemaphoreType.DMA((n,)),
            pltpu.SemaphoreType.DMA((CHUNKS,)),
            pltpu.SemaphoreType.DMA((k, CHUNKS)),
            pltpu.SemaphoreType.DMA((k - 1, CHUNKS)),
            pltpu.SemaphoreType.DMA((k,)),
            pltpu.SemaphoreType.DMA((k,)),
        ],
        compiler_params=pltpu.CompilerParams(
            collective_id=0, has_side_effects=True, vmem_limit_bytes=60 * 1024 * 1024
        ),
    )(cut(slab), factor, top, low, cut(queries))
    return (solved.transpose(1, 0, 2).reshape(rows, width), scores)


def solution(mesh):
    return jax.shard_map(
        local,
        mesh=mesh,
        in_specs=(P("corpus", "feat"), P("feat", "corpus"), P("corpus", "feat")),
        out_specs=(P("corpus", "feat"), P(("corpus", "feat"), None)),
        check_vma=False,
    )
```
